256 devices in a mesh: ctx: 32 (over z, x), head: 8 (over y, core).
Axes of the slice: x: 4, y: 4, z: 8, core: 2. Of those that a mesh axis runs over, the one named last changes fastest.
Arguments:
- query: bfloat16 [32, 2, 128, 8192], P('ctx', None, 'head'), may hold values from -200 to 200
- keyval: bfloat16 [32, 2, 2, 128, 1024], P('ctx', None, None, 'head'), may hold values from -6 to 6
- doc_blocks: int32 [4], replicated, may hold values from 1 to 48, 64 in all
Outputs:
- attended: bfloat16 [32, 2, 128, 8192], P('ctx', None, 'head')
The draws below stay inside these ranges and needn't reach their ends.
Inputs may be any that keep to these rules, and one draw needn't show every extreme that they name: `doc_blocks`: documents fill the sequence in order; the longest has exactly 48 blocks.
All inputs are finite; a program needn't handle non-finite values.
Results may differ from the reference program's by a relative error of at most 0.0038.
Values may be sent and summed in bfloat16 or wider, within the bound.
No kernel may reach another device: no remote copies, remote signals or barrier semaphores. Data moves between devices by JAX's collectives and lax.ppermute only.
A program may use at most 64 MiB of HBM per device.

```python
import math
import jax
import jax.numpy as jnp
import numpy as np
from jax import lax

QUERY_HEADS = 64
KEY_VALUE_HEADS = 8
HEAD_WIDTH = 128
CH = 128
BLK = 128
NDOC = 4
SPANS = 32
PACKED_TOKENS = 8192
SB = 64
MOSTB = 48


def refold_drawn(sequence):
    width = sequence.shape[-1]
    half_len = sequence.shape[0] // 2
    lower_half = sequence[:half_len].reshape(SPANS, CH, width)
    upper_half = jnp.flip(sequence[half_len:].reshape(SPANS, CH, width), axis=0)
    return jnp.stack([lower_half, upper_half], axis=1)


def keys_values(key):
    drawn_sample = jax.random.normal(jax.random.fold_in(key, 11), (2, PACKED_TOKENS, KEY_VALUE_HEADS * HEAD_WIDTH), jnp.float32)
    drawn_sample = jnp.clip(drawn_sample, -5.0, 5.0)
    return drawn_sample


def draw_keyval(key, part):
    drawn_sample = keys_values(key)
    return jnp.stack([refold_drawn(drawn_sample[0]), refold_drawn(drawn_sample[1])], axis=1).astype(jnp.bfloat16)


def draw_query(key, part):
    drawn_sample = jax.random.normal(jax.random.fold_in(key, 21), (PACKED_TOKENS, QUERY_HEADS * HEAD_WIDTH), jnp.float32)
    drawn_sample = jnp.clip(drawn_sample, -5.0, 5.0)
    return refold_drawn(drawn_sample).astype(jnp.bfloat16)


def split_up(number_of, total, reach, skew):
    portions = [(1 << 20) // math.isqrt(grade ** skew) + 1 for grade in range(2, number_of + 1)]
    rest, given = total - reach - (number_of - 1), [1] * (number_of - 1)
    while rest > 0:
        free = [i for i in range(number_of - 1) if given[i] < reach]
        whole, remaining = sum([portions[i] for i in free]), rest
        for i in free:
            addition = min(reach - given[i], max(1, remaining * portions[i] // whole), rest)
            given[i] = given[i] + addition
            rest = rest - addition
    return np.array([reach] + given)


def uneven(key, amount, total, limit, lean):
    if amount == 2:
        one = jax.random.randint(key, (), max(1, total - limit), min(limit, total - 1) + 1)
        return jnp.stack([one, total - one])
    tallies = jnp.asarray(split_up(amount, total, limit, lean), jnp.int32)
    couples = (amount - 1) // 2
    source_of, receiver = tallies[1:1 + 2 * couples:2], tallies[2:2 + 2 * couples:2]
    slack = jnp.minimum(source_of - 1, limit - receiver)
    moved = jax.random.randint(jax.random.fold_in(key, 1), (couples,), 0, 1 << 20) % (slack + 1)
    tallies = tallies.at[1:1 + 2 * couples:2].set(source_of - moved).at[2:2 + 2 * couples:2].set(receiver + moved)
    return tallies[jax.random.permutation(jax.random.fold_in(key, 2), amount)]


def setup_inputs(seed: int = 0) -> dict:
    arg_keys = jax.random.split(jax.random.key(seed), 4)
    query = draw_query(jax.random.fold_in(arg_keys[3], 71), 0)
    keyval = draw_keyval(jax.random.fold_in(arg_keys[3], 71), 0)
    doc_blocks = uneven(arg_keys[2], NDOC, SB, MOSTB, 2).astype(jnp.int32)
    return dict(query=query, keyval=keyval, doc_blocks=doc_blocks)


def unfold(folded):
    width = folded.shape[-1]
    lower_half = folded[:, 0].reshape(-1, width)
    upper_half = jnp.flip(folded[:, 1], axis=0).reshape(-1, width)
    return jnp.concatenate([lower_half, upper_half], axis=0)


def refold(sequence):
    width = sequence.shape[-1]
    half_len = sequence.shape[0] // 2
    lower_half = sequence[:half_len].reshape(SPANS, CH, width)
    upper_half = jnp.flip(sequence[half_len:].reshape(SPANS, CH, width), axis=0)
    return jnp.stack([lower_half, upper_half], axis=1)


def doc_index(positions, doc_ends):
    return jnp.sum((positions[:, None] >= doc_ends[None, :]).astype(jnp.int32), axis=1).astype(jnp.int32)


def reference(query, keyval, doc_blocks):
    queries_seq = unfold(query)
    keys_seq = unfold(keyval[:, 0])
    values_seq = unfold(keyval[:, 1])
    doc_ends = (jnp.cumsum(doc_blocks) * BLK).astype(jnp.int32)
    positions = jnp.arange(PACKED_TOKENS, dtype=jnp.int32)
    doc_ids = doc_index(positions, doc_ends)
    rows_per_block = min(512, PACKED_TOKENS)
    block_count = PACKED_TOKENS // rows_per_block
    heads_per_group = QUERY_HEADS // KEY_VALUE_HEADS
    scale_factor = HEAD_WIDTH ** -0.5

    def one_block(block_no):
        row_start = (block_no * rows_per_block).astype(jnp.int32)
        query_block_size = lax.dynamic_slice_in_dim(queries_seq, row_start, rows_per_block, 0)
        query_block_size = query_block_size.reshape(rows_per_block, KEY_VALUE_HEADS, heads_per_group, HEAD_WIDTH).astype(jnp.float32)
        query_pos = row_start + jnp.arange(rows_per_block, dtype=jnp.int32)
        query_doc = lax.dynamic_slice_in_dim(doc_ids, row_start, rows_per_block, 0)
        visible = (query_doc[:, None] == doc_ids[None, :]) & (positions[None, :] <= query_pos[:, None])

        def single_head(head_no):
            offset = (head_no * HEAD_WIDTH).astype(jnp.int32)
            head_keys = lax.dynamic_slice_in_dim(keys_seq, offset, HEAD_WIDTH, 1).astype(jnp.float32)
            head_values = lax.dynamic_slice_in_dim(values_seq, offset, HEAD_WIDTH, 1).astype(jnp.float32)
            head_q = query_block_size[:, head_no]
            scores = jnp.einsum("rjd,kd->jrk", head_q, head_keys) * scale_factor
            scores = jnp.where(visible[None], scores, -jnp.inf)
            row_max = jnp.max(scores, axis=-1, keepdims=True)
            probs = jnp.exp(scores - row_max)
            totals = jnp.sum(probs, axis=-1, keepdims=True)
            weights = lax.optimization_barrier(probs.astype(jnp.bfloat16)).astype(jnp.float32)
            mixed = jnp.einsum("jrk,kd->jrd", weights, head_values) / totals
            return mixed.astype(jnp.bfloat16)

        head_stack = lax.map(single_head, jnp.arange(KEY_VALUE_HEADS, dtype=jnp.int32))
        return jnp.transpose(head_stack, (2, 0, 1, 3)).reshape(rows_per_block, QUERY_HEADS * HEAD_WIDTH)

    blocks = lax.map(one_block, jnp.arange(block_count, dtype=jnp.int32))
    return refold(blocks.reshape(PACKED_TOKENS, QUERY_HEADS * HEAD_WIDTH))
```

```python
import functools

import jax
import jax.numpy as jnp
from jax import lax
from jax.experimental import pallas as pl
from jax.experimental.pallas import tpu as pltpu
from jax.sharding import Mesh
from jax.sharding import PartitionSpec as P

QUERY_HEADS = 64
KEY_VALUE_HEADS = 8
HEAD_WIDTH = 128
GROUP = QUERY_HEADS // KEY_VALUE_HEADS
BLK = 128
Z, X = 8, 4
SPAN_COUNT = 2 * Z * X
CTX = ("z", "x")
FAR = -1e30
SCALE = HEAD_WIDTH ** (-0.5) * 1.4426950408889634


def attend(count, first, last, info, q_ref, *refs):
    bundles, refs = refs[:count], refs[count:]
    if not first:
        old, refs = refs[:3], refs[3:]
    if last:
        out_ref, refs = refs[0], refs[1:]
    max_ref, sum_ref, acc_ref = refs
    if first:
        max_ref[...] = jnp.full_like(max_ref, FAR)
        sum_ref[...] = jnp.zeros_like(sum_ref)
        acc_ref[...] = jnp.zeros_like(acc_ref)
    elif last:
        for ref, kept in zip(refs, old):
            ref[...] = kept[...]
    tilt = lax.broadcasted_iota(jnp.int32, (BLK, BLK), 1) - lax.broadcasted_iota(
        jnp.int32, (BLK, BLK), 0
    )
    x_index = info[4]

    for number, bundle in enumerate(bundles):
        z_index = info[5 + number]

        def pair(step, _, bundle=bundle, z_index=z_index):
            half, side = step // 2, step % 2
            start, own = info[2 * half], info[2 * half + 1]
            low = jnp.where(side == 0, z_index * X, SPAN_COUNT - X - z_index * X)

            def fold(masked):
                keys = jnp.concatenate([bundle[d, side] for d in range(X)], axis=0)
                values = jnp.concatenate([bundle[d, 2 + side] for d in range(X)], axis=0)
                shown = []
                if masked:
                    for d in range(X):
                        place = lax.rem(x_index - d + X, X)
                        span = low + jnp.where(side == 0, place, X - 1 - place)
                        reach = jnp.where(span >= start, (own - span) * BLK, -2 * BLK)
                        shown.append(tilt <= reach)
                for g in range(GROUP):
                    columns = slice(g * HEAD_WIDTH, (g + 1) * HEAD_WIDTH)
                    rows = jnp.concatenate(
                        [q_ref[src, half, :, columns] for src in range(q_ref.shape[0])], axis=0
                    )
                    scores = (
                        lax.dot_general(
                            rows, keys, (((1,), (1,)), ((), ())), preferred_element_type=jnp.float32
                        )
                        * SCALE
                    )
                    parts = [scores[:, d * BLK : (d + 1) * BLK] for d in range(X)]
                    if masked:
                        parts = [jnp.where(s, part, 2 * FAR) for s, part in zip(shown, parts)]
                    top = functools.reduce(jnp.maximum, parts)
                    before = max_ref[half, g]
                    now = jnp.maximum(before, jnp.max(top, axis=1, keepdims=True))
                    fade = jnp.exp2(before - now)
                    parts = [jnp.exp2(part - now) for part in parts]
                    max_ref[half, g] = now
                    sum_ref[half, g] = sum_ref[half, g] * fade + functools.reduce(jnp.add, parts)
                    weights = jnp.concatenate([part.astype(jnp.bfloat16) for part in parts], axis=1)
                    acc_ref[half, g] = acc_ref[half, g] * fade + jnp.dot(
                        weights, values, preferred_element_type=jnp.float32
                    )

            touched = (low <= own) & (low + X > start)
            whole = (low + X <= own) & (low >= start)
            pl.when(whole)(lambda: fold(False))
            pl.when(touched & jnp.logical_not(whole))(lambda: fold(True))
            return 0

        lax.fori_loop(0, 4, pair, 0)

    if last:
        tokens = out_ref.shape[2]
        for half in range(2):
            for g in range(GROUP):
                totals = jnp.sum(sum_ref[half, g], axis=1, keepdims=True)
                result = (acc_ref[half, g] / totals).astype(jnp.bfloat16)
                for src in range(out_ref.shape[0]):
                    out_ref[src, half, :, g * HEAD_WIDTH : (g + 1) * HEAD_WIDTH] = result[
                        src * tokens : (src + 1) * tokens
                    ]


def run(info, query, bundles, state, last):
    first = state is None
    shape = (2, GROUP, BLK, HEAD_WIDTH)
    vmem = pl.BlockSpec(memory_space=pltpu.VMEM)
    kept = [] if first else list(state)
    if last:
        out_shape = jax.ShapeDtypeStruct(query.shape, jnp.bfloat16)
        out_specs, scratch, aliases = vmem, [pltpu.VMEM(shape, jnp.float32)] * 3, {}
    else:
        out_shape = [jax.ShapeDtypeStruct(shape, jnp.float32)] * 3
        out_specs, scratch = [vmem] * 3, []
        at = 2 + len(bundles)
        aliases = {} if first else {at + i: i for i in range(3)}

    def body(*refs):
        info_ref, q_ref = refs[0], refs[1]
        held = refs[2 : 2 + len(bundles)]
        rest = refs[2 + len(bundles) :]
        attend(len(bundles), first, last, info_ref, q_ref, *held, *rest)

    pairs = 4 * len(bundles)
    return pl.pallas_call(
        body,
        out_shape=out_shape,
        in_specs=[pl.BlockSpec(memory_space=pltpu.SMEM)] + [vmem] * (1 + len(bundles) + len(kept)),
        out_specs=out_specs,
        scratch_shapes=scratch,
        input_output_aliases=aliases,
        compiler_params=pltpu.CompilerParams(vmem_limit_bytes=40 * 2**20),
        cost_estimate=pl.CostEstimate(
            flops=pairs * 4 * 1024 * 512 * 128, bytes_accessed=2**22, transcendentals=pairs * 2**19
        ),
    )(info, query, *bundles, *kept)


def shift(x, axis, size, by):
    return lax.ppermute(x, axis, [(i, (i + by) % size) for i in range(size)])


def local(query, keyval, doc_blocks):
    z, x = lax.axis_index("z"), lax.axis_index("x")
    c = z * X + x
    tokens = keyval.shape[3]
    sources = BLK // tokens
    kv = keyval.reshape(4, tokens, KEY_VALUE_HEADS, HEAD_WIDTH).transpose(2, 0, 1, 3)
    kv = lax.all_to_all(kv, "head", split_axis=0, concat_axis=0, tiled=True)
    kv = kv.transpose(1, 0, 2, 3).reshape(4, BLK, HEAD_WIDTH)
    bundle = jnp.stack([kv] + [shift(kv, "x", X, d) for d in range(1, X)])

    q = query.reshape(2, tokens, KEY_VALUE_HEADS, GROUP * HEAD_WIDTH).transpose(2, 0, 1, 3)
    q = lax.all_to_all(q, "head", split_axis=0, concat_axis=0, tiled=True)

    ends, total = [], jnp.int32(0)
    for j in range(doc_blocks.shape[0]):
        total = total + doc_blocks[j]
        ends.append(total)
    head = []
    for span in (c, SPAN_COUNT - 1 - c):
        start = jnp.int32(0)
        for end in ends:
            start = jnp.maximum(start, jnp.where(end <= span, end, 0))
        head += [start, span]

    def info(*places):
        return jnp.stack([jnp.asarray(v, jnp.int32) for v in (*head, x, *places)])

    up = down = bundle
    state = run(info(z), q, [bundle], None, False)
    for k in range(1, Z // 2):
        up, down = shift(up, "z", Z, 1), shift(down, "z", Z, -1)
        state = run(info((z - k) % Z, (z + k) % Z), q, [up, down], state, False)
    up = shift(up, "z", Z, 1)
    out = run(info((z - Z // 2) % Z), q, [up], state, True)

    out = lax.all_to_all(out, "head", split_axis=0, concat_axis=0, tiled=True)
    return out.transpose(1, 2, 0, 3).reshape(query.shape)


def solution(mesh):
    torus = Mesh(mesh.devices.reshape(Z, X, mesh.shape["head"]), ("z", "x", "head"))
    placed = (P(CTX, None, "head", None), P(CTX, None, None, "head", None), P())
    return jax.shard_map(
        local, mesh=torus, in_specs=placed, out_specs=P(CTX, None, "head", None), check_vma=False
    )
```

```python
import functools

import jax
import jax.numpy as jnp
from jax import lax
from jax.experimental import pallas as pl
from jax.experimental.pallas import tpu as pltpu
from jax.sharding import Mesh
from jax.sharding import PartitionSpec as P

QUERY_HEADS = 64
KEY_VALUE_HEADS = 8
HEAD_WIDTH = 128
GROUP = QUERY_HEADS // KEY_VALUE_HEADS
BLK = 128
Z, X = 8, 4
SPAN_COUNT = 2 * Z * X
CTX = ("z", "x")
FAR = -1e30
ORDER = (0, 1, 3, 2)
SCALE = HEAD_WIDTH ** (-0.5) * 1.4426950408889634


def attend(count, first, last, info, q_ref, *refs):
    bundles, refs = refs[: 2 * count], refs[2 * count :]
    if not first:
        old, refs = refs[:3], refs[3:]
    if last:
        out_ref, refs = refs[0], refs[1:]
    max_ref, sum_ref, acc_ref = refs[:3]
    if first:
        rows_ref = refs[3]
        sources, _, tokens, _ = q_ref.shape
        for half in range(2):
            for g in range(GROUP):
                for src in range(sources):
                    rows_ref[half, g, src * tokens : (src + 1) * tokens] = q_ref[
                        src, half, :, g * HEAD_WIDTH : (g + 1) * HEAD_WIDTH
                    ]
        max_ref[...] = jnp.full_like(max_ref, FAR)
        sum_ref[...] = jnp.zeros_like(sum_ref)
        acc_ref[...] = jnp.zeros_like(acc_ref)
    else:
        rows_ref = q_ref
        if last:
            for ref, kept in zip(refs, old):
                ref[...] = kept[...]
    tilt = lax.broadcasted_iota(jnp.int32, (BLK, BLK), 1) - lax.broadcasted_iota(
        jnp.int32, (BLK, BLK), 0
    )
    x_index = info[4]

    for number in range(count):
        blocks = [(ref, i) for ref in bundles[2 * number : 2 * number + 2] for i in range(2)]

        def pair(step, _, blocks=blocks, z_index=info[5 + number]):
            half, side = step // 2, step % 2
            start, own = info[2 * half], info[2 * half + 1]
            low = jnp.where(side == 0, z_index * X, SPAN_COUNT - X - z_index * X)

            def fold(masked):
                keys = jnp.concatenate([ref[i, side] for ref, i in blocks], axis=0)
                values = jnp.concatenate([ref[i, 2 + side] for ref, i in blocks], axis=0)
                rows = rows_ref[half].reshape(GROUP * BLK, HEAD_WIDTH)
                scores = (
                    lax.dot_general(
                        rows, keys, (((1,), (1,)), ((), ())), preferred_element_type=jnp.float32
                    )
                    * SCALE
                )
                parts = [
                    scores[:, d * BLK : (d + 1) * BLK].reshape(GROUP, BLK, BLK) for d in range(X)
                ]
                if masked:
                    for d in range(X):
                        place = lax.rem(x_index - ORDER[d] + X, X)
                        span = low + jnp.where(side == 0, place, X - 1 - place)
                        reach = jnp.where(span >= start, (own - span) * BLK, -2 * BLK)
                        parts[d] = jnp.where((tilt <= reach)[None], parts[d], 2 * FAR)
                top = functools.reduce(jnp.maximum, parts)
                before = max_ref[half]
                now = jnp.maximum(before, jnp.max(top, axis=2, keepdims=True))
                fade = jnp.exp2(before - now)
                parts = [jnp.exp2(part - now) for part in parts]
                max_ref[half] = now
                sum_ref[half] = sum_ref[half] * fade + functools.reduce(jnp.add, parts)
                weights = jnp.concatenate([part.astype(jnp.bfloat16) for part in parts], axis=2)
                added = jnp.dot(
                    weights.reshape(GROUP * BLK, X * BLK), values, preferred_element_type=jnp.float32
                )
                acc_ref[half] = acc_ref[half] * fade + added.reshape(GROUP, BLK, HEAD_WIDTH)

            touched = (low <= own) & (low + X > start)
            whole = (low + X <= own) & (low >= start)
            pl.when(whole)(lambda: fold(False))
            pl.when(touched & jnp.logical_not(whole))(lambda: fold(True))
            return 0

        lax.fori_loop(0, 4, pair, 0)

    if last:
        tokens = out_ref.shape[2]
        for half in range(2):
            for g in range(GROUP):
                totals = jnp.sum(sum_ref[half, g], axis=1, keepdims=True)
                result = (acc_ref[half, g] / totals).astype(jnp.bfloat16)
                for src in range(out_ref.shape[0]):
                    out_ref[src, half, :, g * HEAD_WIDTH : (g + 1) * HEAD_WIDTH] = result[
                        src * tokens : (src + 1) * tokens
                    ]


def run(info, query, bundles, state, last, shape=None):
    first = state is None
    state_shape = (2, GROUP, BLK, HEAD_WIDTH)
    vmem = pl.BlockSpec(memory_space=pltpu.VMEM)
    kept = [] if first else list(state)
    refs = len(bundles)
    if last:
        out_shape = jax.ShapeDtypeStruct(shape, jnp.bfloat16)
        out_specs, scratch, aliases = vmem, [pltpu.VMEM(state_shape, jnp.float32)] * 3, {}
    else:
        out_shape = [jax.ShapeDtypeStruct(state_shape, jnp.float32)] * 3
        if first:
            out_shape.append(jax.ShapeDtypeStruct(state_shape, jnp.bfloat16))
        out_specs, scratch = [vmem] * len(out_shape), []
        aliases = {} if first else {2 + refs + i: i for i in range(3)}
    pairs = 2 * refs
    return pl.pallas_call(
        functools.partial(attend, refs // 2, first, last),
        out_shape=out_shape,
        in_specs=[pl.BlockSpec(memory_space=pltpu.SMEM)] + [vmem] * (1 + refs + len(kept)),
        out_specs=out_specs,
        scratch_shapes=scratch,
        input_output_aliases=aliases,
        compiler_params=pltpu.CompilerParams(vmem_limit_bytes=24 * 2**20),
        cost_estimate=pl.CostEstimate(
            flops=pairs * 4 * 1024 * 512 * 128, bytes_accessed=2**22, transcendentals=pairs * 2**19
        ),
    )(info, query, *bundles, *kept)


def shift(x, axis, size, by):
    return lax.ppermute(x, axis, [(i, (i + by) % size) for i in range(size)])


def local(query, keyval, doc_blocks):
    z, x = lax.axis_index("z"), lax.axis_index("x")
    c = z * X + x
    tokens = keyval.shape[3]
    sources = BLK // tokens
    kv = keyval.reshape(4, tokens, KEY_VALUE_HEADS, HEAD_WIDTH).transpose(2, 0, 1, 3)
    kv = lax.all_to_all(kv, "head", split_axis=0, concat_axis=0, tiled=True)
    kv = kv.transpose(1, 0, 2, 3).reshape(4, BLK, HEAD_WIDTH)
    near = jnp.stack([kv, shift(kv, "x", X, ORDER[1])])
    rest = jnp.stack([shift(kv, "x", X, ORDER[2]), shift(kv, "x", X, ORDER[3])])

    q = query.reshape(2, tokens, KEY_VALUE_HEADS, GROUP * HEAD_WIDTH).transpose(2, 0, 1, 3)
    q = lax.all_to_all(q, "head", split_axis=0, concat_axis=0, tiled=True)

    shape = q.shape

    ends, total = [], jnp.int32(0)
    for j in range(doc_blocks.shape[0]):
        total = total + doc_blocks[j]
        ends.append(total)
    head = []
    for span in (c, SPAN_COUNT - 1 - c):
        start = jnp.int32(0)
        for end in ends:
            start = jnp.maximum(start, jnp.where(end <= span, end, 0))
        head += [start, span]

    def info(*places):
        return jnp.stack([jnp.asarray(v, jnp.int32) for v in (*head, x, *places)])

    *state, q = run(info(z), q, [near, rest], None, False)
    up0 = down0 = near
    up1 = down1 = rest
    for k in range(1, Z // 2):
        up0, down0 = shift(up0, "z", Z, 1), shift(down0, "z", Z, -1)
        up1, down1 = shift(up1, "z", Z, 1), shift(down1, "z", Z, -1)
        (up1, down1), state = lax.optimization_barrier(((up1, down1), state))
        state = run(info((z - k) % Z, (z + k) % Z), q, [up0, up1, down0, down1], state, False)
    up0, down1 = shift(up0, "z", Z, 1), shift(down1, "z", Z, -1)
    out = run(info((z - Z // 2) % Z), q, [up0, down1], state, True, shape)

    out = lax.all_to_all(out, "head", split_axis=0, concat_axis=0, tiled=True)
    return out.transpose(1, 2, 0, 3).reshape(query.shape)


def solution(mesh):
    torus = Mesh(mesh.devices.reshape(Z, X, mesh.shape["head"]), ("z", "x", "head"))
    placed = (P(CTX, None, "head", None), P(CTX, None, None, "head", None), P())
    return jax.shard_map(
        local, mesh=torus, in_specs=placed, out_specs=P(CTX, None, "head", None), check_vma=False
    )
```

```python
import functools

import jax
import jax.numpy as jnp
from jax import lax
from jax.experimental import pallas as pl
from jax.experimental.pallas import tpu as pltpu
from jax.sharding import Mesh
from jax.sharding import PartitionSpec as P

QUERY_HEADS = 64
KEY_VALUE_HEADS = 8
HEAD_WIDTH = 128
GROUP = QUERY_HEADS // KEY_VALUE_HEADS
BLK = 128
Z, X = 8, 4
SPAN_COUNT = 2 * Z * X
CTX = ("z", "x")
FAR = -1e30
ORDER = (0, 1, 3, 2)
SCALE = HEAD_WIDTH ** (-0.5) * 1.4426950408889634


def attend(steps, count, first, last, docs_ref, rows_ref, *refs):
    sent, refs = refs[:count], refs[count:]
    if not first:
        old, refs = refs[:3], refs[3:]
    if last:
        out_ref, refs = refs[0], refs[1:]
    max_ref, sum_ref, acc_ref = refs[:3]
    if first:
        sent_ref, rows_ref = rows_ref, refs[3]
        tokens = sent_ref.shape[2]
        for src in range(sent_ref.shape[0]):
            for g in range(GROUP):
                for half in range(2):
                    rows_ref[half, g, src * tokens : (src + 1) * tokens] = sent_ref[src, 2 * g + half]
        max_ref[...] = jnp.full_like(max_ref, FAR)
        sum_ref[...] = jnp.zeros_like(sum_ref)
        acc_ref[...] = jnp.zeros_like(acc_ref)
    elif last:
        for ref, kept in zip(refs[:3], old):
            ref[...] = kept[...]
    tilt = lax.broadcasted_iota(jnp.int32, (BLK, BLK), 1) - lax.broadcasted_iota(
        jnp.int32, (BLK, BLK), 0
    )
    my_z, x_index = lax.axis_index("z"), lax.axis_index("x")
    place = my_z * X + x_index
    owns = (place, SPAN_COUNT - 1 - place)
    starts = [jnp.int32(0), jnp.int32(0)]
    end = jnp.int32(0)
    for j in range(docs_ref.shape[0]):
        end = end + docs_ref[j]
        starts = [jnp.where(end <= own, end, start) for own, start in zip(owns, starts)]

    for away, picks in steps:
        blocks = [sent[array].at[i] for array, i in picks]
        z_index = lax.rem(my_z + away + Z, Z)

        def pair(step, _, blocks=blocks, z_index=z_index):
            half, side = step // 2, step % 2
            start = jnp.where(half == 0, starts[0], starts[1])
            own = jnp.where(half == 0, owns[0], owns[1])
            low = jnp.where(side == 0, z_index * X, SPAN_COUNT - X - z_index * X)

            def fold(masked):
                keys = jnp.concatenate([ref[side] for ref in blocks], axis=0)
                values = jnp.concatenate([ref[2 + side] for ref in blocks], axis=0)
                rows = rows_ref[half].reshape(GROUP * BLK, HEAD_WIDTH)
                scores = (
                    lax.dot_general(
                        rows, keys, (((1,), (1,)), ((), ())), preferred_element_type=jnp.float32
                    )
                    * SCALE
                )
                parts = [
                    scores[:, d * BLK : (d + 1) * BLK].reshape(GROUP, BLK, BLK) for d in range(X)
                ]
                if masked:
                    for d in range(X):
                        place = lax.rem(x_index - ORDER[d] + X, X)
                        span = low + jnp.where(side == 0, place, X - 1 - place)
                        reach = jnp.where(span >= start, (own - span) * BLK, -2 * BLK)
                        parts[d] = jnp.where((tilt <= reach)[None], parts[d], 2 * FAR)
                top = functools.reduce(jnp.maximum, parts)
                before = max_ref[half]
                now = jnp.maximum(before, jnp.max(top, axis=2, keepdims=True))
                fade = jnp.exp2(before - now)
                parts = [jnp.exp2(part - now) for part in parts]
                max_ref[half] = now
                sum_ref[half] = sum_ref[half] * fade + functools.reduce(jnp.add, parts)
                weights = jnp.concatenate([part.astype(jnp.bfloat16) for part in parts], axis=2)
                added = jnp.dot(
                    weights.reshape(GROUP * BLK, X * BLK), values, preferred_element_type=jnp.float32
                )
                acc_ref[half] = acc_ref[half] * fade + added.reshape(GROUP, BLK, HEAD_WIDTH)

            touched = (low <= own) & (low + X > start)
            whole = (low + X <= own) & (low >= start)
            pl.when(whole)(lambda: fold(False))
            pl.when(touched & jnp.logical_not(whole))(lambda: fold(True))
            return 0

        lax.fori_loop(0, 4, pair, 0)

    if last:
        tokens = out_ref.shape[2]
        for half in range(2):
            for g in range(GROUP):
                totals = jnp.sum(sum_ref[half, g], axis=1, keepdims=True)
                result = (acc_ref[half, g] / totals).astype(jnp.bfloat16)
                for src in range(out_ref.shape[0]):
                    out_ref[src, half, :, g * HEAD_WIDTH : (g + 1) * HEAD_WIDTH] = result[
                        src * tokens : (src + 1) * tokens
                    ]


def run(doc_blocks, query, steps, bundles, state, last, shape=None):
    first = state is None
    state_shape = (2, GROUP, BLK, HEAD_WIDTH)
    vmem = pl.BlockSpec(memory_space=pltpu.VMEM)
    kept = [] if first else list(state)
    refs = len(bundles)
    if last:
        out_shape = jax.ShapeDtypeStruct(shape, jnp.bfloat16)
        out_specs, scratch, aliases = vmem, [pltpu.VMEM(state_shape, jnp.float32)] * 3, {}
    else:
        out_shape = [jax.ShapeDtypeStruct(state_shape, jnp.float32)] * 3
        if first:
            out_shape.append(jax.ShapeDtypeStruct(state_shape, jnp.bfloat16))
        out_specs, scratch = [vmem] * len(out_shape), []
        aliases = {} if first else {2 + refs + i: i for i in range(3)}
    pairs = 4 * len(steps)
    return pl.pallas_call(
        functools.partial(attend, steps, refs, first, last),
        out_shape=out_shape,
        in_specs=[pl.BlockSpec(memory_space=pltpu.SMEM)] + [vmem] * (1 + refs + len(kept)),
        out_specs=out_specs,
        scratch_shapes=scratch,
        input_output_aliases=aliases,
        compiler_params=pltpu.CompilerParams(vmem_limit_bytes=20 * 2**20),
        cost_estimate=pl.CostEstimate(
            flops=pairs * 4 * 1024 * 512 * 128, bytes_accessed=2**22, transcendentals=pairs * 2**19
        ),
    )(doc_blocks, query, *bundles, *kept)


def moved(moves, operands, shapes):
    left = pl.BlockSpec(memory_space=pl.ANY)

    def body(*refs):
        ins, outs, sem = refs[: len(operands)], refs[len(operands) : -1], refs[-1]
        copies = [
            pltpu.make_async_copy(ins[i].at[src], outs[o].at[dst], sem.at[n])
            for n, (i, src, o, dst) in enumerate(moves)
        ]
        for copy in copies:
            copy.start()
        for copy in copies:
            copy.wait()

    return pl.pallas_call(
        body,
        out_shape=[jax.ShapeDtypeStruct(shape, jnp.bfloat16) for shape in shapes],
        in_specs=[left] * len(operands),
        out_specs=[left] * len(shapes),
        scratch_shapes=[pltpu.SemaphoreType.DMA((len(moves),))],
        compiler_params=pltpu.CompilerParams(vmem_limit_bytes=2**20),
        cost_estimate=pl.CostEstimate(flops=0, bytes_accessed=2**20, transcendentals=0),
    )(*operands)


def pack(in_ref, out_ref):
    heads, parts, _, width = out_ref.shape
    lead = in_ref.shape[0]
    for h in range(heads):
        for part in range(parts):
            at = (h * (parts // lead) + part // lead) * width
            out_ref[h, part] = in_ref[part % lead, :, at : at + width]


def unpack(in_ref, out_ref):
    tokens = in_ref.shape[2]
    for src in range(in_ref.shape[0]):
        for j in range(in_ref.shape[1]):
            out_ref[0, j, src * tokens : (src + 1) * tokens] = in_ref[src, j]


def arranged(body, operands, shapes):
    vmem = pl.BlockSpec(memory_space=pltpu.VMEM)
    return pl.pallas_call(
        body,
        out_shape=[jax.ShapeDtypeStruct(shape, jnp.bfloat16) for shape in shapes],
        in_specs=[vmem] * len(operands),
        out_specs=[vmem] * len(shapes),
        compiler_params=pltpu.CompilerParams(vmem_limit_bytes=8 * 2**20),
        cost_estimate=pl.CostEstimate(flops=0, bytes_accessed=2**20, transcendentals=0),
    )(*operands)


def shift(x, axis, size, by):
    return lax.ppermute(x, axis, [(i, (i + by) % size) for i in range(size)])


def exchange(x):
    return lax.all_to_all(x, "head", split_axis=0, concat_axis=0, tiled=True)


def local(query, keyval, doc_blocks):
    tokens = keyval.shape[3]
    wide = GROUP * HEAD_WIDTH
    every = slice(None)
    heads = KEY_VALUE_HEADS
    kv = keyval.reshape(4, tokens, heads * HEAD_WIDTH)
    [kv] = arranged(pack, [kv], [(heads, 4, tokens, HEAD_WIDTH)])
    [near] = arranged(unpack, [exchange(kv)], [(1, 4, BLK, HEAD_WIDTH)])
    q = query.reshape(2, tokens, heads * wide)
    [q] = arranged(pack, [q], [(heads, 2 * GROUP, tokens, HEAD_WIDTH)])
    q = exchange(q)
    shape = (heads, 2, tokens, wide)
    beside = [shift(near, "x", X, d) for d in ORDER[1:3]]
    far = shift(near, "x", X, ORDER[3])
    block = near.shape[1:]
    [trio] = moved([(i, 0, 0, i) for i in range(3)], [near, *beside], [(3, *block)])

    picks = [(0, 0), (0, 1), (0, 2), (1, 0)]
    *state, q = run(doc_blocks, q, [(0, picks)], [trio, far], None, False)
    up = down = trio
    for k in range(1, Z // 2):
        up, down = shift(up, "z", Z, 1), shift(down, "z", Z, -1)
        both = [(0, 2, 0, 0), (1, 2, 0, 1)]
        if k < Z // 2 - 1:
            [cross] = moved(both, [up, down], [(2, *block)])
        else:
            cross, pair, lone = moved(
                [*both, (0, pl.ds(0, 2), 1, every), (1, 2, 2, 0)],
                [up, down],
                [(2, *block), (2, *block), (1, *block)],
            )
        cross = shift(cross, "x", X, -1)
        picks = [[(side, 0), (side, 1), (side, 2), (2, side)] for side in range(2)]
        steps = [(-k, picks[0]), (k, picks[1])]
        if k > 1:
            (up, down), state = lax.optimization_barrier(((up, down), state))
        state = run(doc_blocks, q, steps, [up, down, cross], state, False)
    pair, lone = shift(pair, "z", Z, 1), shift(lone, "z", Z, -1)
    cross = shift(lone, "x", X, -1)
    picks = [(0, 0), (0, 1), (1, 0), (2, 0)]
    out = run(doc_blocks, q, [(-(Z // 2), picks)], [pair, lone, cross], state, True, shape)

    out = exchange(out)
    [out] = moved(
        [(0, h, 0, (every, every, pl.ds(h * wide, wide))) for h in range(KEY_VALUE_HEADS)],
        [out],
        [(2, tokens, KEY_VALUE_HEADS * wide)],
    )
    return out.reshape(query.shape)


def solution(mesh):
    torus = Mesh(mesh.devices.reshape(Z, X, mesh.shape["head"]), ("z", "x", "head"))
    placed = (P(CTX, None, "head", None), P(CTX, None, None, "head", None), P())
    return jax.shard_map(
        local, mesh=torus, in_specs=placed, out_specs=P(CTX, None, "head", None), check_vma=False
    )
```

```python
import functools

import jax
import jax.numpy as jnp
from jax import lax
from jax.experimental import pallas as pl
from jax.experimental.pallas import tpu as pltpu
from jax.sharding import Mesh
from jax.sharding import PartitionSpec as P

QUERY_HEADS = 64
KEY_VALUE_HEADS = 8
HEAD_WIDTH = 128
GROUP = QUERY_HEADS // KEY_VALUE_HEADS
BLK = 128
Z, X = 8, 4
SPAN_COUNT = 2 * Z * X
CTX = ("z", "x")
FAR = -1e30
ORDER = (0, 1, 3, 2)
SCALE = HEAD_WIDTH ** (-0.5) * 1.4426950408889634


def attend(steps, count, first, last, docs_ref, rows_ref, *refs):
    sent, refs = refs[:count], refs[count:]
    if not first:
        refs = refs[3:]
    if last:
        out_ref, refs = refs[0], refs[1:]
    max_ref, sum_ref, acc_ref = refs[:3]
    if first:
        sent_ref, rows_ref = rows_ref, refs[3]
        tokens = sent_ref.shape[2]
        for src in range(sent_ref.shape[0]):
            for g in range(GROUP):
                for half in range(2):
                    rows_ref[half, g, src * tokens : (src + 1) * tokens] = sent_ref[src, 2 * g + half]
        max_ref[...] = jnp.full_like(max_ref, FAR)
        sum_ref[...] = jnp.zeros_like(sum_ref)
        acc_ref[...] = jnp.zeros_like(acc_ref)
    tilt = lax.broadcasted_iota(jnp.int32, (BLK, BLK), 1) - lax.broadcasted_iota(
        jnp.int32, (BLK, BLK), 0
    )
    my_z, x_index = lax.axis_index("z"), lax.axis_index("x")
    place = my_z * X + x_index
    owns = (place, SPAN_COUNT - 1 - place)
    starts = [jnp.int32(0), jnp.int32(0)]
    end = jnp.int32(0)
    for j in range(docs_ref.shape[0]):
        end = end + docs_ref[j]
        starts = [jnp.where(end <= own, end, start) for own, start in zip(owns, starts)]

    for away, picks in steps:
        blocks = [sent[array].at[i] for array, i in picks]
        z_index = lax.rem(my_z + away + Z, Z)

        def pair(step, _, blocks=blocks, z_index=z_index):
            half, side = step // 2, step % 2
            start = jnp.where(half == 0, starts[0], starts[1])
            own = jnp.where(half == 0, owns[0], owns[1])
            low = jnp.where(side == 0, z_index * X, SPAN_COUNT - X - z_index * X)

            def fold(masked):
                keys = jnp.concatenate([ref[side] for ref in blocks], axis=0)
                values = jnp.concatenate([ref[2 + side] for ref in blocks], axis=0)
                rows = rows_ref[half].reshape(GROUP * BLK, HEAD_WIDTH)
                scores = lax.dot_general(
                    rows, keys, (((1,), (1,)), ((), ())), preferred_element_type=jnp.float32
                )
                parts = [
                    scores[:, d * BLK : (d + 1) * BLK].reshape(GROUP, BLK, BLK) for d in range(X)
                ]
                if masked:
                    for d in range(X):
                        place = lax.rem(x_index - ORDER[d] + X, X)
                        span = low + jnp.where(side == 0, place, X - 1 - place)
                        reach = jnp.where(span >= start, (own - span) * BLK, -2 * BLK)
                        parts[d] = jnp.where((tilt <= reach)[None], parts[d], 2 * FAR)
                top = functools.reduce(jnp.maximum, parts)
                before = max_ref[half]
                now = jnp.maximum(before, jnp.max(top, axis=2, keepdims=True))
                fade = jnp.exp2((before - now) * SCALE)
                parts = [jnp.exp2((part - now) * SCALE) for part in parts]
                max_ref[half] = now
                sum_ref[half] = sum_ref[half] * fade + functools.reduce(jnp.add, parts)
                weights = jnp.concatenate([part.astype(jnp.bfloat16) for part in parts], axis=2)
                added = jnp.dot(
                    weights.reshape(GROUP * BLK, X * BLK), values, preferred_element_type=jnp.float32
                )
                acc_ref[half] = acc_ref[half] * fade + added.reshape(GROUP, BLK, HEAD_WIDTH)

            touched = (low <= own) & (low + X > start)
            whole = (low + X <= own) & (low >= start)
            pl.when(whole)(lambda: fold(False))
            pl.when(touched & jnp.logical_not(whole))(lambda: fold(True))
            return 0

        lax.fori_loop(0, 4, pair, 0)

    if last:
        tokens = out_ref.shape[2]
        for half in range(2):
            for g in range(GROUP):
                totals = jnp.sum(sum_ref[half, g], axis=1, keepdims=True)
                result = (acc_ref[half, g] / totals).astype(jnp.bfloat16)
                for src in range(out_ref.shape[0]):
                    out_ref[src, half, :, g * HEAD_WIDTH : (g + 1) * HEAD_WIDTH] = result[
                        src * tokens : (src + 1) * tokens
                    ]


def run(doc_blocks, query, steps, bundles, state, last, shape=None):
    first = state is None
    state_shape = (2, GROUP, BLK, HEAD_WIDTH)
    vmem = pl.BlockSpec(memory_space=pltpu.VMEM)
    kept = [] if first else list(state)
    refs = len(bundles)
    out_shape = [jax.ShapeDtypeStruct(state_shape, jnp.float32)] * 3
    at, offset = 2 + refs, 1 if last else 0
    aliases = {} if first else {at + i: offset + i for i in range(3)}
    if first:
        out_shape = [*out_shape, jax.ShapeDtypeStruct(state_shape, jnp.bfloat16)]
    if last:
        out_shape = [jax.ShapeDtypeStruct(shape, jnp.bfloat16), *out_shape]
    pairs = 4 * len(steps)
    return pl.pallas_call(
        functools.partial(attend, steps, refs, first, last),
        out_shape=out_shape,
        in_specs=[pl.BlockSpec(memory_space=pltpu.SMEM)] + [vmem] * (1 + refs + len(kept)),
        out_specs=[vmem] * len(out_shape),
        input_output_aliases=aliases,
        compiler_params=pltpu.CompilerParams(vmem_limit_bytes=20 * 2**20),
        cost_estimate=pl.CostEstimate(
            flops=pairs * 4 * 1024 * 512 * 128, bytes_accessed=2**22, transcendentals=pairs * 2**19
        ),
    )(doc_blocks, query, *bundles, *kept)


def moved(moves, operands, shapes):
    left = pl.BlockSpec(memory_space=pl.ANY)

    def body(*refs):
        ins, outs, sem = refs[: len(operands)], refs[len(operands) : -1], refs[-1]
        copies = [
            pltpu.make_async_copy(ins[i].at[src], outs[o].at[dst], sem.at[n])
            for n, (i, src, o, dst) in enumerate(moves)
        ]
        for copy in copies:
            copy.start()
        for copy in copies:
            copy.wait()

    return pl.pallas_call(
        body,
        out_shape=[jax.ShapeDtypeStruct(shape, jnp.bfloat16) for shape in shapes],
        in_specs=[left] * len(operands),
        out_specs=[left] * len(shapes),
        scratch_shapes=[pltpu.SemaphoreType.DMA((len(moves),))],
        compiler_params=pltpu.CompilerParams(vmem_limit_bytes=2**20),
        cost_estimate=pl.CostEstimate(flops=0, bytes_accessed=2**20, transcendentals=0),
    )(*operands)


def pack(in_ref, out_ref):
    heads, parts, _, width = out_ref.shape
    lead = in_ref.shape[0]
    for h in range(heads):
        for part in range(parts):
            at = (h * (parts // lead) + part // lead) * width
            out_ref[h, part] = in_ref[part % lead, :, at : at + width]


def unpack(in_ref, out_ref):
    tokens = in_ref.shape[2]
    for src in range(in_ref.shape[0]):
        for j in range(in_ref.shape[1]):
            out_ref[0, j, src * tokens : (src + 1) * tokens] = in_ref[src, j]


def arranged(body, operands, shapes):
    vmem = pl.BlockSpec(memory_space=pltpu.VMEM)
    return pl.pallas_call(
        body,
        out_shape=[jax.ShapeDtypeStruct(shape, jnp.bfloat16) for shape in shapes],
        in_specs=[vmem] * len(operands),
        out_specs=[vmem] * len(shapes),
        compiler_params=pltpu.CompilerParams(vmem_limit_bytes=8 * 2**20),
        cost_estimate=pl.CostEstimate(flops=0, bytes_accessed=2**20, transcendentals=0),
    )(*operands)


def shift(x, axis, size, by):
    return lax.ppermute(x, axis, [(i, (i + by) % size) for i in range(size)])


def exchange(x):
    return lax.all_to_all(x, "head", split_axis=0, concat_axis=0, tiled=True)


def local(query, keyval, doc_blocks):
    tokens = keyval.shape[3]
    wide = GROUP * HEAD_WIDTH
    every = slice(None)
    heads = KEY_VALUE_HEADS
    kv = keyval.reshape(4, tokens, heads * HEAD_WIDTH)
    [kv] = arranged(pack, [kv], [(heads, 4, tokens, HEAD_WIDTH)])
    [near] = arranged(unpack, [exchange(kv)], [(1, 4, BLK, HEAD_WIDTH)])
    q = query.reshape(2, tokens, heads * wide)
    [q] = arranged(pack, [q], [(heads, 2 * GROUP, tokens, HEAD_WIDTH)])
    q = exchange(q)
    shape = (heads, 2, tokens, wide)
    beside = [shift(near, "x", X, d) for d in ORDER[1:3]]
    far = shift(near, "x", X, ORDER[3])
    block = near.shape[1:]
    [trio] = moved([(i, 0, 0, i) for i in range(3)], [near, *beside], [(3, *block)])

    picks = [(0, 0), (0, 1), (0, 2), (1, 0)]
    up, down = shift(trio, "z", Z, 1), shift(trio, "z", Z, -1)
    (up, down), q, far = lax.optimization_barrier(((up, down), q, far))
    *state, q = run(doc_blocks, q, [(0, picks)], [trio, far], None, False)
    for k in range(1, Z // 2):
        both = [(0, 2, 0, 0), (1, 2, 0, 1)]
        if k < Z // 2 - 1:
            [cross] = moved(both, [up, down], [(2, *block)])
            ahead, behind = up, down
        else:
            cross, ahead, behind = moved(
                [*both, (0, pl.ds(0, 2), 1, every), (1, 2, 2, 0)],
                [up, down],
                [(2, *block), (2, *block), (1, *block)],
            )
        following = shift(ahead, "z", Z, 1), shift(behind, "z", Z, -1)
        cross = shift(cross, "x", X, -1)
        picks = [[(side, 0), (side, 1), (side, 2), (2, side)] for side in range(2)]
        steps = [(-k, picks[0]), (k, picks[1])]
        following, state = lax.optimization_barrier((following, state))
        state = run(doc_blocks, q, steps, [up, down, cross], state, False)
        up, down = following
    cross = shift(down, "x", X, -1)
    picks = [(0, 0), (0, 1), (1, 0), (2, 0)]
    out, *_ = run(doc_blocks, q, [(-(Z // 2), picks)], [up, down, cross], state, True, shape)

    out = exchange(out)
    [out] = moved(
        [(0, h, 0, (every, every, pl.ds(h * wide, wide))) for h in range(KEY_VALUE_HEADS)],
        [out],
        [(2, tokens, KEY_VALUE_HEADS * wide)],
    )
    return out.reshape(query.shape)


def solution(mesh):
    torus = Mesh(mesh.devices.reshape(Z, X, mesh.shape["head"]), ("z", "x", "head"))
    placed = (P(CTX, None, "head", None), P(CTX, None, None, "head", None), P())
    return jax.shard_map(
        local, mesh=torus, in_specs=placed, out_specs=P(CTX, None, "head", None), check_vma=False
    )
```

```python
import functools

import jax
import jax.numpy as jnp
from jax import lax
from jax.experimental import pallas as pl
from jax.experimental.pallas import tpu as pltpu
from jax.sharding import Mesh
from jax.sharding import PartitionSpec as P

QUERY_HEADS = 64
KEY_VALUE_HEADS = 8
HEAD_WIDTH = 128
GROUP = QUERY_HEADS // KEY_VALUE_HEADS
BLK = 128
Z, X = 8, 4
SPAN_COUNT = 2 * Z * X
CTX = ("z", "x")
FAR = -1e30
WIDE = 2
ORDER = (0, 1, 3, 2)
SCALE = HEAD_WIDTH ** (-0.5) * 1.4426950408889634


def attend(steps, count, first, last, docs_ref, rows_ref, *refs):
    sent, refs = refs[:count], refs[count:]
    if not first:
        refs = refs[3:]
    if last:
        out_ref, refs = refs[0], refs[1:]
    max_ref, sum_ref, acc_ref = refs[:3]
    if first:
        sent_ref, rows_ref = rows_ref, refs[3]
        tokens = sent_ref.shape[2]
        for src in range(sent_ref.shape[0]):
            for g in range(GROUP):
                for half in range(2):
                    rows_ref[half, g, src * tokens : (src + 1) * tokens] = sent_ref[src, 2 * g + half]
        max_ref[...] = jnp.full_like(max_ref, FAR)
        sum_ref[...] = jnp.zeros_like(sum_ref)
        acc_ref[...] = jnp.zeros_like(acc_ref)
    tilt = lax.broadcasted_iota(jnp.int32, (BLK, BLK), 1) - lax.broadcasted_iota(
        jnp.int32, (BLK, BLK), 0
    )
    my_z, x_index = lax.axis_index("z"), lax.axis_index("x")
    place = my_z * X + x_index
    owns = (place, SPAN_COUNT - 1 - place)
    starts = [jnp.int32(0), jnp.int32(0)]
    end = jnp.int32(0)
    for j in range(docs_ref.shape[0]):
        end = end + docs_ref[j]
        starts = [jnp.where(end <= own, end, start) for own, start in zip(owns, starts)]

    chips = [
        (lax.rem(my_z + away + Z, Z), [sent[array].at[i] for array, i in picks])
        for away, picks in steps
    ]

    def pair(step, _):
        half, side = step // 2, step % 2
        start = jnp.where(half == 0, starts[0], starts[1])
        own = jnp.where(half == 0, owns[0], owns[1])

        def fold(blocks, chunk, low=None):
            keys = jnp.concatenate([ref[side] for ref in blocks], axis=0)
            values = jnp.concatenate([ref[2 + side] for ref in blocks], axis=0)
            chunks = [pl.ds(g, chunk) for g in range(0, GROUP, chunk)]
            scores = [
                lax.dot_general(
                    rows_ref[half, at].reshape(chunk * BLK, HEAD_WIDTH),
                    keys,
                    (((1,), (1,)), ((), ())),
                    preferred_element_type=jnp.float32,
                )
                for at in chunks
            ]
            folded = []
            for at, score in zip(chunks, scores):
                parts = [
                    score[:, d * BLK : (d + 1) * BLK].reshape(chunk, BLK, BLK)
                    for d in range(len(blocks))
                ]
                if low is not None:
                    for d in range(X):
                        place = lax.rem(x_index - ORDER[d] + X, X)
                        span = low + jnp.where(side == 0, place, X - 1 - place)
                        reach = jnp.where(span >= start, (own - span) * BLK, -2 * BLK)
                        parts[d] = jnp.where((tilt <= reach)[None], parts[d], 2 * FAR)
                top = functools.reduce(jnp.maximum, parts)
                before = max_ref[half, at]
                now = jnp.maximum(before, jnp.max(top, axis=2, keepdims=True))
                fade = jnp.exp2((before - now) * SCALE)
                parts = [jnp.exp2((part - now) * SCALE) for part in parts]
                max_ref[half, at] = now
                sum_ref[half, at] = sum_ref[half, at] * fade + functools.reduce(jnp.add, parts)
                weights = jnp.concatenate([part.astype(jnp.bfloat16) for part in parts], axis=2)
                folded.append((fade, weights.reshape(chunk * BLK, len(blocks) * BLK)))
            for at, (fade, weights) in zip(chunks, folded):
                added = jnp.dot(weights, values, preferred_element_type=jnp.float32)
                acc_ref[half, at] = acc_ref[half, at] * fade + added.reshape(
                    chunk, BLK, HEAD_WIDTH
                )

        lows = [
            jnp.where(side == 0, z_index * X, SPAN_COUNT - X - z_index * X) for z_index, _ in chips
        ]
        wholes = [(low + X <= own) & (low >= start) for low in lows]
        every = functools.reduce(jnp.logical_and, wholes)
        if len(chips) > 1:
            pl.when(every)(lambda: fold([ref for _, blocks in chips for ref in blocks], WIDE))
        for (_, blocks), low, whole in zip(chips, lows, wholes):
            touched = (low <= own) & (low + X > start)
            alone = whole & jnp.logical_not(every) if len(chips) > 1 else whole
            pl.when(alone)(lambda blocks=blocks: fold(blocks, GROUP))
            pl.when(touched & jnp.logical_not(whole))(
                lambda blocks=blocks, low=low: fold(blocks, GROUP, low)
            )
        return 0

    lax.fori_loop(0, 4, pair, 0)

    if last:
        tokens = out_ref.shape[2]
        for half in range(2):
            for g in range(GROUP):
                totals = jnp.sum(sum_ref[half, g], axis=1, keepdims=True)
                result = (acc_ref[half, g] / totals).astype(jnp.bfloat16)
                for src in range(out_ref.shape[0]):
                    out_ref[src, half, :, g * HEAD_WIDTH : (g + 1) * HEAD_WIDTH] = result[
                        src * tokens : (src + 1) * tokens
                    ]


def run(doc_blocks, query, steps, bundles, state, last, shape=None):
    first = state is None
    state_shape = (2, GROUP, BLK, HEAD_WIDTH)
    vmem = pl.BlockSpec(memory_space=pltpu.VMEM)
    kept = [] if first else list(state)
    refs = len(bundles)
    out_shape = [jax.ShapeDtypeStruct(state_shape, jnp.float32)] * 3
    at, offset = 2 + refs, 1 if last else 0
    aliases = {} if first else {at + i: offset + i for i in range(3)}
    if first:
        out_shape = [*out_shape, jax.ShapeDtypeStruct(state_shape, jnp.bfloat16)]
    if last:
        out_shape = [jax.ShapeDtypeStruct(shape, jnp.bfloat16), *out_shape]
    pairs = 4 * len(steps)
    return pl.pallas_call(
        functools.partial(attend, steps, refs, first, last),
        out_shape=out_shape,
        in_specs=[pl.BlockSpec(memory_space=pltpu.SMEM)] + [vmem] * (1 + refs + len(kept)),
        out_specs=[vmem] * len(out_shape),
        input_output_aliases=aliases,
        compiler_params=pltpu.CompilerParams(vmem_limit_bytes=20 * 2**20),
        cost_estimate=pl.CostEstimate(
            flops=pairs * 4 * 1024 * 512 * 128, bytes_accessed=2**22, transcendentals=pairs * 2**19
        ),
    )(doc_blocks, query, *bundles, *kept)


def moved(moves, operands, shapes, amount=None):
    left = pl.BlockSpec(memory_space=pl.ANY)
    amount = amount or len(moves)

    def body(*refs):
        ins, outs, sem = refs[: len(operands)], refs[len(operands) : -1], refs[-1]
        head = lax.axis_index("head")
        listed = moves(lax.div(head, 2), lax.rem(head, 2)) if callable(moves) else moves
        copies = [
            pltpu.make_async_copy(ins[i].at[src], outs[o].at[dst], sem.at[n])
            for n, (i, src, o, dst) in enumerate(listed)
        ]
        for copy in copies:
            copy.start()
        for copy in copies:
            copy.wait()

    return pl.pallas_call(
        body,
        out_shape=[jax.ShapeDtypeStruct(shape, jnp.bfloat16) for shape in shapes],
        in_specs=[left] * len(operands),
        out_specs=[left] * len(shapes),
        scratch_shapes=[pltpu.SemaphoreType.DMA((amount,))],
        compiler_params=pltpu.CompilerParams(vmem_limit_bytes=2**20),
        cost_estimate=pl.CostEstimate(flops=0, bytes_accessed=2**20, transcendentals=0),
    )(*operands)


def pack(in_ref, out_ref):
    heads, parts, _, width = out_ref.shape
    lead = in_ref.shape[0]
    for h in range(heads):
        for part in range(parts):
            at = (h * (parts // lead) + part // lead) * width
            out_ref[h, part] = in_ref[part % lead, :, at : at + width]


def unpack(in_ref, out_ref):
    tokens = in_ref.shape[2]
    for src in range(in_ref.shape[0]):
        for j in range(in_ref.shape[1]):
            out_ref[0, j, src * tokens : (src + 1) * tokens] = in_ref[src, j]


def arranged(body, operands, shapes):
    vmem = pl.BlockSpec(memory_space=pltpu.VMEM)
    return pl.pallas_call(
        body,
        out_shape=[jax.ShapeDtypeStruct(shape, jnp.bfloat16) for shape in shapes],
        in_specs=[vmem] * len(operands),
        out_specs=[vmem] * len(shapes),
        compiler_params=pltpu.CompilerParams(vmem_limit_bytes=8 * 2**20),
        cost_estimate=pl.CostEstimate(flops=0, bytes_accessed=2**20, transcendentals=0),
    )(*operands)


def shift(x, axis, size, by):
    return lax.ppermute(x, axis, [(i, (i + by) % size) for i in range(size)])


def returned(out):
    heads, _, tokens, wide = out.shape
    chips = heads // 2
    every = slice(None)

    def onward(y, to):
        return lax.rem(y + to + chips, chips)

    def across(y, core):
        return [(0, 2 * to + 1 - core, 0, to) for to in range(chips)]

    [other] = moved(across, [out], [(chips, *out.shape[1:])], chips)
    other = lax.ppermute(other, "head", [(h, h ^ 1) for h in range(heads)])

    def along(y, core):
        listed = []
        for to in range(1, chips):
            at = onward(y, to)
            listed += [(0, 2 * at + core, to - 1, core), (1, at, to - 1, 1 - core)]
        return listed

    pairs = moved(along, [out, other], [(2, *out.shape[1:])] * (chips - 1), 2 * (chips - 1))
    came = {
        to: lax.ppermute(
            pairs[to - 1], "head", [(h, (h + 2 * to) % heads) for h in range(heads)]
        )
        for to in (2, 1, 3)
    }

    def placed(y, core):
        def columns(head):
            return (every, every, pl.ds(pl.multiple_of(head * wide, wide), wide))

        listed = [
            (0, 2 * y + core, 0, columns(2 * y + core)),
            (1, y, 0, columns(2 * y + 1 - core)),
        ]
        for to in range(1, chips):
            home = onward(y, -to)
            listed += [(1 + to, e, 0, columns(2 * home + e)) for e in range(2)]
        return listed

    arrays = [out, other, *(came[to] for to in range(1, chips))]
    [out] = moved(placed, arrays, [(2, tokens, heads * wide)], heads)
    return out


def exchange(x):
    return lax.all_to_all(x, "head", split_axis=0, concat_axis=0, tiled=True)


def local(query, keyval, doc_blocks):
    tokens = keyval.shape[3]
    wide = GROUP * HEAD_WIDTH
    every = slice(None)
    heads = KEY_VALUE_HEADS
    kv = keyval.reshape(4, tokens, heads * HEAD_WIDTH)
    [kv] = arranged(pack, [kv], [(heads, 4, tokens, HEAD_WIDTH)])
    [near] = arranged(unpack, [exchange(kv)], [(1, 4, BLK, HEAD_WIDTH)])
    q = query.reshape(2, tokens, heads * wide)
    [q] = arranged(pack, [q], [(heads, 2 * GROUP, tokens, HEAD_WIDTH)])
    q = exchange(q)
    shape = (heads, 2, tokens, wide)
    beside = [shift(near, "x", X, d) for d in ORDER[1:3]]
    far = shift(near, "x", X, ORDER[3])
    block = near.shape[1:]
    [trio] = moved([(i, 0, 0, i) for i in range(3)], [near, *beside], [(3, *block)])

    picks = [(0, 0), (0, 1), (0, 2), (1, 0)]
    up, down = shift(trio, "z", Z, 1), shift(trio, "z", Z, -1)
    (up, down), q, far = lax.optimization_barrier(((up, down), q, far))
    *state, q = run(doc_blocks, q, [(0, picks)], [trio, far], None, False)
    for k in range(1, Z // 2):
        both = [(0, 2, 0, 0), (1, 2, 0, 1)]
        if k < Z // 2 - 1:
            [cross] = moved(both, [up, down], [(2, *block)])
            ahead, behind = up, down
        else:
            cross, ahead, behind = moved(
                [*both, (0, pl.ds(0, 2), 1, every), (1, 2, 2, 0)],
                [up, down],
                [(2, *block), (2, *block), (1, *block)],
            )
        following = shift(ahead, "z", Z, 1), shift(behind, "z", Z, -1)
        cross = shift(cross, "x", X, -1)
        picks = [[(side, 0), (side, 1), (side, 2), (2, side)] for side in range(2)]
        steps = [(-k, picks[0]), (k, picks[1])]
        following, state = lax.optimization_barrier((following, state))
        state = run(doc_blocks, q, steps, [up, down, cross], state, False)
        up, down = following
    cross = shift(down, "x", X, -1)
    picks = [(0, 0), (0, 1), (1, 0), (2, 0)]
    out, *_ = run(doc_blocks, q, [(-(Z // 2), picks)], [up, down, cross], state, True, shape)

    out = returned(out)
    return out.reshape(query.shape)


def solution(mesh):
    torus = Mesh(mesh.devices.reshape(Z, X, mesh.shape["head"]), ("z", "x", "head"))
    placed = (P(CTX, None, "head", None), P(CTX, None, None, "head", None), P())
    return jax.shard_map(
        local, mesh=torus, in_specs=placed, out_specs=P(CTX, None, "head", None), check_vma=False
    )
```

```python
import functools

import jax
import jax.numpy as jnp
from jax import lax
from jax.experimental import pallas as pl
from jax.experimental.pallas import tpu as pltpu
from jax.sharding import Mesh
from jax.sharding import PartitionSpec as P

QUERY_HEADS = 64
KEY_VALUE_HEADS = 8
HEAD_WIDTH = 128
GROUP = QUERY_HEADS // KEY_VALUE_HEADS
BLK = 128
Z, X = 8, 4
SPAN_COUNT = 2 * Z * X
CTX = ("z", "x")
FAR = -1e30
WIDE = 4
ORDER = (0, 1, 3, 2)
SCALE = HEAD_WIDTH ** (-0.5) * 1.4426950408889634


def attend(steps, count, first, last, docs_ref, rows_ref, *refs):
    sent, refs = refs[:count], refs[count:]
    if not first:
        refs = refs[3:]
    if last:
        out_ref, refs = refs[0], refs[1:]
    max_ref, sum_ref, acc_ref = refs[:3]
    if first:
        sent_ref, rows_ref = rows_ref, refs[3]
        tokens = sent_ref.shape[2]
        for src in range(sent_ref.shape[0]):
            for g in range(GROUP):
                for half in range(2):
                    rows_ref[half, g, src * tokens : (src + 1) * tokens] = sent_ref[src, 2 * g + half]
        max_ref[...] = jnp.full_like(max_ref, FAR)
        sum_ref[...] = jnp.zeros_like(sum_ref)
        acc_ref[...] = jnp.zeros_like(acc_ref)
    tilt = lax.broadcasted_iota(jnp.int32, (BLK, BLK), 1) - lax.broadcasted_iota(
        jnp.int32, (BLK, BLK), 0
    )
    my_z, x_index = lax.axis_index("z"), lax.axis_index("x")
    place = my_z * X + x_index
    owns = (place, SPAN_COUNT - 1 - place)
    starts = [jnp.int32(0), jnp.int32(0)]
    end = jnp.int32(0)
    for j in range(docs_ref.shape[0]):
        end = end + docs_ref[j]
        starts = [jnp.where(end <= own, end, start) for own, start in zip(owns, starts)]

    chips = [
        (lax.rem(my_z + away + Z, Z), [sent[array].at[i] for array, i in picks])
        for away, picks in steps
    ]

    def pair(step, _):
        half, side = step // 2, step % 2
        start = jnp.where(half == 0, starts[0], starts[1])
        own = jnp.where(half == 0, owns[0], owns[1])

        def fold(blocks, chunk, low=None):
            keys = jnp.concatenate([ref[side] for ref in blocks], axis=0)
            values = jnp.concatenate([ref[2 + side] for ref in blocks], axis=0)
            chunks = [pl.ds(g, chunk) for g in range(0, GROUP, chunk)]
            scores = [
                lax.dot_general(
                    rows_ref[half, at].reshape(chunk * BLK, HEAD_WIDTH),
                    keys,
                    (((1,), (1,)), ((), ())),
                    preferred_element_type=jnp.float32,
                )
                for at in chunks
            ]
            folded = []
            for at, score in zip(chunks, scores):
                parts = [
                    score[:, d * BLK : (d + 1) * BLK].reshape(chunk, BLK, BLK)
                    for d in range(len(blocks))
                ]
                if low is not None:
                    for d in range(X):
                        place = lax.rem(x_index - ORDER[d] + X, X)
                        span = low + jnp.where(side == 0, place, X - 1 - place)
                        reach = jnp.where(span >= start, (own - span) * BLK, -2 * BLK)
                        parts[d] = jnp.where((tilt <= reach)[None], parts[d], 2 * FAR)
                top = functools.reduce(jnp.maximum, parts)
                before = max_ref[half, at]
                now = jnp.maximum(before, jnp.max(top, axis=2, keepdims=True))
                fade = jnp.exp2((before - now) * SCALE)
                parts = [jnp.exp2((part - now) * SCALE) for part in parts]
                max_ref[half, at] = now
                sum_ref[half, at] = sum_ref[half, at] * fade + functools.reduce(jnp.add, parts)
                weights = jnp.concatenate([part.astype(jnp.bfloat16) for part in parts], axis=2)
                folded.append((fade, weights.reshape(chunk * BLK, len(blocks) * BLK)))
            for at, (fade, weights) in zip(chunks, folded):
                added = jnp.dot(weights, values, preferred_element_type=jnp.float32)
                acc_ref[half, at] = acc_ref[half, at] * fade + added.reshape(
                    chunk, BLK, HEAD_WIDTH
                )

        lows = [
            jnp.where(side == 0, z_index * X, SPAN_COUNT - X - z_index * X) for z_index, _ in chips
        ]
        wholes = [(low + X <= own) & (low >= start) for low in lows]
        every = functools.reduce(jnp.logical_and, wholes)
        if len(chips) > 1:
            pl.when(every)(lambda: fold([ref for _, blocks in chips for ref in blocks], WIDE))
        for (_, blocks), low, whole in zip(chips, lows, wholes):
            touched = (low <= own) & (low + X > start)
            alone = whole & jnp.logical_not(every) if len(chips) > 1 else whole
            pl.when(alone)(lambda blocks=blocks: fold(blocks, GROUP))
            pl.when(touched & jnp.logical_not(whole))(
                lambda blocks=blocks, low=low: fold(blocks, GROUP, low)
            )
        return 0

    lax.fori_loop(0, 4, pair, 0)

    if last:
        tokens = out_ref.shape[2]
        for half in range(2):
            for g in range(GROUP):
                totals = jnp.sum(sum_ref[half, g], axis=1, keepdims=True)
                result = (acc_ref[half, g] / totals).astype(jnp.bfloat16)
                for src in range(out_ref.shape[0]):
                    out_ref[src, half, :, g * HEAD_WIDTH : (g + 1) * HEAD_WIDTH] = result[
                        src * tokens : (src + 1) * tokens
                    ]


def run(doc_blocks, query, steps, bundles, state, last, shape=None):
    first = state is None
    state_shape = (2, GROUP, BLK, HEAD_WIDTH)
    vmem = pl.BlockSpec(memory_space=pltpu.VMEM)
    kept = [] if first else list(state)
    refs = len(bundles)
    out_shape = [jax.ShapeDtypeStruct(state_shape, jnp.float32)] * 3
    at, offset = 2 + refs, 1 if last else 0
    aliases = {} if first else {at + i: offset + i for i in range(3)}
    if first:
        out_shape = [*out_shape, jax.ShapeDtypeStruct(state_shape, jnp.bfloat16)]
    if last:
        out_shape = [jax.ShapeDtypeStruct(shape, jnp.bfloat16), *out_shape]
    pairs = 4 * len(steps)
    return pl.pallas_call(
        functools.partial(attend, steps, refs, first, last),
        out_shape=out_shape,
        in_specs=[pl.BlockSpec(memory_space=pltpu.SMEM)] + [vmem] * (1 + refs + len(kept)),
        out_specs=[vmem] * len(out_shape),
        input_output_aliases=aliases,
        compiler_params=pltpu.CompilerParams(vmem_limit_bytes=20 * 2**20),
        cost_estimate=pl.CostEstimate(
            flops=pairs * 4 * 1024 * 512 * 128, bytes_accessed=2**22, transcendentals=pairs * 2**19
        ),
    )(doc_blocks, query, *bundles, *kept)


def moved(moves, operands, shapes, amount=None):
    left = pl.BlockSpec(memory_space=pl.ANY)
    amount = amount or len(moves)

    def body(*refs):
        ins, outs, sem = refs[: len(operands)], refs[len(operands) : -1], refs[-1]
        head = lax.axis_index("head")
        listed = moves(lax.div(head, 2), lax.rem(head, 2)) if callable(moves) else moves
        copies = [
            pltpu.make_async_copy(ins[i].at[src], outs[o].at[dst], sem.at[n])
            for n, (i, src, o, dst) in enumerate(listed)
        ]
        for copy in copies:
            copy.start()
        for copy in copies:
            copy.wait()

    return pl.pallas_call(
        body,
        out_shape=[jax.ShapeDtypeStruct(shape, jnp.bfloat16) for shape in shapes],
        in_specs=[left] * len(operands),
        out_specs=[left] * len(shapes),
        scratch_shapes=[pltpu.SemaphoreType.DMA((amount,))],
        compiler_params=pltpu.CompilerParams(vmem_limit_bytes=2**20),
        cost_estimate=pl.CostEstimate(flops=0, bytes_accessed=2**20, transcendentals=0),
    )(*operands)


def pack(in_ref, out_ref):
    heads, parts, _, width = out_ref.shape
    lead = in_ref.shape[0]
    for h in range(heads):
        for part in range(parts):
            at = (h * (parts // lead) + part // lead) * width
            out_ref[h, part] = in_ref[part % lead, :, at : at + width]


def unpack(in_ref, out_ref):
    tokens = in_ref.shape[2]
    for src in range(in_ref.shape[0]):
        for j in range(in_ref.shape[1]):
            out_ref[0, j, src * tokens : (src + 1) * tokens] = in_ref[src, j]


def arranged(body, operands, shapes):
    vmem = pl.BlockSpec(memory_space=pltpu.VMEM)
    return pl.pallas_call(
        body,
        out_shape=[jax.ShapeDtypeStruct(shape, jnp.bfloat16) for shape in shapes],
        in_specs=[vmem] * len(operands),
        out_specs=[vmem] * len(shapes),
        compiler_params=pltpu.CompilerParams(vmem_limit_bytes=8 * 2**20),
        cost_estimate=pl.CostEstimate(flops=0, bytes_accessed=2**20, transcendentals=0),
    )(*operands)


def shift(x, axis, size, by):
    return lax.ppermute(x, axis, [(i, (i + by) % size) for i in range(size)])


def returned(out):
    heads, _, tokens, wide = out.shape
    chips = heads // 2
    every = slice(None)

    def onward(y, to):
        return lax.rem(y + to + chips, chips)

    def across(y, core):
        return [(0, 2 * to + 1 - core, 0, to) for to in range(chips)]

    [other] = moved(across, [out], [(chips, *out.shape[1:])], chips)
    other = lax.ppermute(other, "head", [(h, h ^ 1) for h in range(heads)])

    def along(y, core):
        listed = []
        for to in range(1, chips):
            at = onward(y, to)
            listed += [(0, 2 * at + core, to - 1, core), (1, at, to - 1, 1 - core)]
        return listed

    pairs = moved(along, [out, other], [(2, *out.shape[1:])] * (chips - 1), 2 * (chips - 1))
    came = {
        to: lax.ppermute(
            pairs[to - 1], "head", [(h, (h + 2 * to) % heads) for h in range(heads)]
        )
        for to in (2, 1, 3)
    }

    def placed(y, core):
        def columns(head):
            return (every, every, pl.ds(pl.multiple_of(head * wide, wide), wide))

        listed = [
            (0, 2 * y + core, 0, columns(2 * y + core)),
            (1, y, 0, columns(2 * y + 1 - core)),
        ]
        for to in range(1, chips):
            home = onward(y, -to)
            listed += [(1 + to, e, 0, columns(2 * home + e)) for e in range(2)]
        return listed

    arrays = [out, other, *(came[to] for to in range(1, chips))]
    [out] = moved(placed, arrays, [(2, tokens, heads * wide)], heads)
    return out


def exchange(x):
    return lax.all_to_all(x, "head", split_axis=0, concat_axis=0, tiled=True)


def local(query, keyval, doc_blocks):
    tokens = keyval.shape[3]
    wide = GROUP * HEAD_WIDTH
    every = slice(None)
    heads = KEY_VALUE_HEADS
    kv = keyval.reshape(4, tokens, heads * HEAD_WIDTH)
    [kv] = arranged(pack, [kv], [(heads, 4, tokens, HEAD_WIDTH)])
    [near] = arranged(unpack, [exchange(kv)], [(1, 4, BLK, HEAD_WIDTH)])
    q = query.reshape(2, tokens, heads * wide)
    [q] = arranged(pack, [q], [(heads, 2 * GROUP, tokens, HEAD_WIDTH)])
    q = exchange(q)
    shape = (heads, 2, tokens, wide)
    beside = [shift(near, "x", X, d) for d in ORDER[1:3]]
    far = shift(near, "x", X, ORDER[3])
    block = near.shape[1:]
    [trio] = moved([(i, 0, 0, i) for i in range(3)], [near, *beside], [(3, *block)])

    picks = [(0, 0), (0, 1), (0, 2), (1, 0)]
    up, down = shift(trio, "z", Z, 1), shift(trio, "z", Z, -1)
    (up, down), q, far = lax.optimization_barrier(((up, down), q, far))
    *state, q = run(doc_blocks, q, [(0, picks)], [trio, far], None, False)
    for k in range(1, Z // 2):
        both = [(0, 2, 0, 0), (1, 2, 0, 1)]
        if k < Z // 2 - 1:
            [cross] = moved(both, [up, down], [(2, *block)])
            ahead, behind = up, down
        else:
            cross, ahead, behind = moved(
                [*both, (0, pl.ds(0, 2), 1, every), (1, 2, 2, 0)],
                [up, down],
                [(2, *block), (2, *block), (1, *block)],
            )
        back = shift(behind, "z", Z, -1)
        following = shift(ahead, "z", Z, 1), back
        cross = shift(cross, "x", X, -1)
        picks = [[(side, 0), (side, 1), (side, 2), (2, side)] for side in range(2)]
        steps = [(-k, picks[0]), (k, picks[1])]
        following, state = lax.optimization_barrier((following, state))
        state = run(doc_blocks, q, steps, [up, down, cross], state, False)
        up, down = following
    cross = shift(down, "x", X, -1)
    picks = [(0, 0), (0, 1), (1, 0), (2, 0)]
    out, *_ = run(doc_blocks, q, [(-(Z // 2), picks)], [up, down, cross], state, True, shape)

    out = returned(out)
    return out.reshape(query.shape)


def solution(mesh):
    torus = Mesh(mesh.devices.reshape(Z, X, mesh.shape["head"]), ("z", "x", "head"))
    placed = (P(CTX, None, "head", None), P(CTX, None, None, "head", None), P())
    return jax.shard_map(
        local, mesh=torus, in_specs=placed, out_specs=P(CTX, None, "head", None), check_vma=False
    )
```
